32 devices in a mesh: seq: 8 (over z, core), tensor: 4 (over y, x).
Axes of the slice: x: 2, y: 2, z: 4, core: 2. Of those that a mesh axis runs over, the one named last changes fastest.
Arguments:
- queries: bfloat16 [3, 24, 40, 5120], P(None, 'seq', None, 'tensor'), may hold values from -16 to 16
- keys_values: bfloat16 [2, 3, 24, 40, 5120], P(None, None, 'seq', None, 'tensor'), may hold values from -16 to 16
- out_weight: bfloat16 [5120, 5120], P('tensor'), may hold values from -0.078125 to 0.078125
- grad_out: bfloat16 [3, 24, 40, 5120], P(None, 'seq', 'tensor'), may hold values from -6 to 6
- window: int32 [40, 3], P('tensor'), may hold values from 0 to 3, as said below
- block_mask: int32 [1, 8, 5, 63], replicated, may hold values from 0 to 1, as said below
Outputs:
- layer_out: bfloat16 [3, 24, 40, 5120], P(None, 'seq', 'tensor')
- grad_queries: bfloat16 [3, 24, 40, 5120], P(None, 'seq', None, 'tensor')
- grad_keys_values: bfloat16 [2, 3, 24, 40, 5120], P(None, None, 'seq', None, 'tensor')
- grad_weight: bfloat16 [5120, 5120], P('tensor', 'seq')
The draws below stay inside these ranges and needn't reach their ends.
Inputs may be any that keep to these rules, and one draw needn't show every extreme that they name: `window`: in every group of 10 consecutive heads one head has the reach (1, 1, 3). `block_mask`: the middle entry of every tile's row (the tile itself) is 1.
All inputs are finite; a program needn't handle non-finite values.
Results may differ from the reference program's by a relative error of at most 0.014.
Values may be sent and summed in bfloat16 or wider, within the bound.
A program may use at most 128 MiB of HBM per device.

```python
import jax
import jax.numpy as jnp
from jax import lax

D = 5120
HEADS = 40
HEAD_DIM = 128
FRAMES = 3
COLUMNS = 40
TILE_F = 3
TILE_H = 3
TILE_W = 8
REACH_F = 1
REACH_H = 1
REACH_W = 3
OFFSETS = 63
HEADS_DEV = 10
HEIGHT = 24
FRAME_TILES = 1
ROW_TILES = 8
COL_TILES = 5
N_SEQ = 8
N_TENSOR = 4


def base_values(key, salt):
    folded = jax.random.fold_in(key, salt)
    shape = (FRAMES, HEIGHT, COLUMNS, D)
    return jnp.clip(jax.random.normal(jax.random.fold_in(folded, 3), shape, jnp.float32), -6.0, 6.0)


def draw_queries(key, part):
    drawn_draw = base_values(key, 1)
    return drawn_draw.astype(jnp.bfloat16)


def draw_keys_values(key, part):
    key_draw = base_values(key, 2)
    values = base_values(key, 3)
    return jnp.stack([key_draw, values]).astype(jnp.bfloat16)


def draw_window(key, part):
    reaches = jnp.stack([jax.random.randint(jax.random.fold_in(key, 1), (HEADS,), 0, REACH_F + 1), jax.random.randint(jax.random.fold_in(key, 2), (HEADS,), 0, REACH_H + 1), jax.random.randint(jax.random.fold_in(key, 3), (HEADS,), 0, REACH_W + 1)], axis=1)
    chosen_slot = jax.random.randint(jax.random.fold_in(key, 4), (HEADS // HEADS_DEV,), 0, HEADS_DEV)
    head_slots = jnp.arange(HEADS, dtype=jnp.int32)
    chosen = head_slots % HEADS_DEV == jnp.repeat(chosen_slot, HEADS_DEV)
    widest = jnp.array([REACH_F, REACH_H, REACH_W], jnp.int32)
    return jnp.where(chosen[:, None], widest[None, :], reaches).astype(jnp.int32)


def draw_block_mask(key, part):
    mask_bits = jax.random.randint(jax.random.fold_in(key, 5), (FRAME_TILES, ROW_TILES, COL_TILES, OFFSETS), 0, 2)
    middle = jnp.arange(OFFSETS, dtype=jnp.int32) == OFFSETS // 2
    return jnp.where(middle, 1, mask_bits).astype(jnp.int32)


def raised(drawn, key, source, target, parts, factor):
    def block_of(axis_at):
        return (jnp.arange(drawn.shape[axis_at]) // (drawn.shape[axis_at] // parts)).reshape((-1,) + (1,) * (drawn.ndim - 1 - axis_at))

    one_side = jax.random.permutation(key, parts)[block_of(target)]
    other_side = (block_of(target) + parts // 2) % parts
    return jnp.where((block_of(source) == one_side) | (block_of(source) == other_side), factor * drawn, drawn)


def levels(key, dims, split, smallest, high):
    factor_of, own = 1.0, jax.random.fold_in(key, 6)
    for axis_at, blocks in split:
        steps = jnp.exp(jax.random.uniform(jax.random.fold_in(own, axis_at), (blocks,), jnp.float32, smallest / len(split), high / len(split)))
        factor_of = factor_of * jnp.repeat(steps, dims[axis_at] // blocks).reshape([-1 if axis == axis_at else 1 for axis in range(len(dims))])
    return factor_of


def gaussian(key, shape, width, limit, split=(), kind=jnp.bfloat16):
    result = jax.random.normal(key, shape, jnp.float32) * width
    if len(split) > 0:
        result = levels(key, shape, split, -0.22, 0.18) * result
    return jnp.clip(result, min=-limit, max=limit).astype(kind)


def heavy_noise(rng, extent, scale, reach, shards, heavy, kind=jnp.bfloat16):
    entries = scale * jax.random.normal(rng, extent, jnp.float32)
    if shards:
        entries = entries * levels(rng, extent, shards, -0.22, 0.18)
    return jnp.clip(raised(entries, jax.random.fold_in(rng, 3), *heavy), -reach, reach).astype(kind)


def setup_inputs(seed: int = 0) -> dict:
    splits = jax.random.split(jax.random.key(seed), 7)
    return {
        "queries": draw_queries(jax.random.fold_in(splits[6], 71), 0),
        "keys_values": draw_keys_values(jax.random.fold_in(splits[6], 71), 0),
        "out_weight": gaussian(splits[2], (D, D), D ** -0.5, 0.078125, ((0, 4),)),
        "grad_out": heavy_noise(splits[3], (FRAMES, HEIGHT, COLUMNS, D), 1.0, 6.0, ((1, 8), (2, 4)), (1, 3, 8, 2.0)),
        "window": draw_window(jax.random.fold_in(splits[6], 71), 0),
        "block_mask": draw_block_mask(jax.random.fold_in(splits[6], 71), 0),
    }


def product(left, right):
    return jnp.dot(left.astype(jnp.float32), right.astype(jnp.float32), preferred_element_type=jnp.float32)


def tile_order(grid):
    frames, height, columns, channels = grid.shape
    shaped = grid.reshape(frames // TILE_F, TILE_F, height // TILE_H, TILE_H, columns // TILE_W, TILE_W, channels)
    return shaped.transpose(0, 2, 4, 1, 3, 5, 6).reshape(-1, channels)


def grid_order(flat_rows, frames, height, columns):
    channels = flat_rows.shape[-1]
    shaped = flat_rows.reshape(frames // TILE_F, height // TILE_H, columns // TILE_W, TILE_F, TILE_H, TILE_W, channels)
    return shaped.transpose(0, 3, 1, 4, 2, 5, 6).reshape(frames, height, columns, channels)


def tile_coords(frames, height, columns, first_row):
    frame_count = frames // TILE_F
    row_count = height // TILE_H
    column_count = columns // TILE_W
    linear = jnp.arange(frame_count * row_count * column_count, dtype=jnp.int32)
    return (linear // (row_count * column_count), linear // column_count % row_count + first_row, linear % column_count)


def allowed_mask(reach_row, mask_rows, query_tiles, key_tiles, row_tiles):
    delta_f = key_tiles[0][None, :] - query_tiles[0][:, None]
    delta_h = key_tiles[1][None, :] - query_tiles[1][:, None]
    delta_w = key_tiles[2][None, :] - query_tiles[2][:, None]
    inside = (jnp.abs(delta_f) <= reach_row[0]) & (jnp.abs(delta_h) <= reach_row[1]) & (jnp.abs(delta_w) <= reach_row[2])
    inside = inside & ((key_tiles[1] >= 0) & (key_tiles[1] < row_tiles))[None, :]
    offset = ((delta_f + REACH_F) * (2 * REACH_H + 1) + delta_h + REACH_H) * (2 * REACH_W + 1) + delta_w + REACH_W
    mask_bits = jnp.sum(jnp.where(offset[:, :, None] == jnp.arange(OFFSETS, dtype=jnp.int32), mask_rows[:, None, :], 0), axis=-1)
    tiles_ok = inside & (mask_bits > 0)
    tile_size = TILE_F * TILE_H * TILE_W
    query_count, key_count = tiles_ok.shape
    spread = jnp.broadcast_to(tiles_ok[:, None, :, None], (query_count, tile_size, key_count, tile_size))
    return spread.reshape(query_count * tile_size, key_count * tile_size)


def head_forward(q_rows, k_rows, v_rows, allowed):
    scores = product(q_rows, k_rows.T) * HEAD_DIM ** -0.5
    scores = jnp.where(allowed, scores, -jnp.inf)
    row_max = jnp.max(scores, axis=1)
    weights = jnp.exp(scores - row_max[:, None])
    row_sum = jnp.sum(weights, axis=1)
    probs = weights / row_sum[:, None]
    attended = product(probs.astype(jnp.bfloat16), v_rows).astype(jnp.bfloat16)
    return attended, row_max, row_sum


def head_backward(q_rows, k_rows, v_rows, grad_rows, allowed, row_max, row_sum):
    scores = product(q_rows, k_rows.T) * HEAD_DIM ** -0.5
    scores = jnp.where(allowed, scores, -jnp.inf)
    probs = jnp.exp(scores - row_max[:, None]) / row_sum[:, None]
    rounded = probs.astype(jnp.bfloat16)
    grad_values = product(rounded.T, grad_rows)
    grad_probs = product(grad_rows, v_rows.T)
    row_delta = jnp.sum(probs * grad_probs, axis=1)
    grad_scores = (probs * (grad_probs - row_delta[:, None]) * HEAD_DIM ** -0.5).astype(jnp.bfloat16)
    return product(grad_scores, k_rows), product(grad_scores.T, q_rows), grad_values


def reference(queries, keys_values, out_weight, grad_out, window, block_mask):
    frames, height, columns, model_width = queries.shape
    padded_kv = jnp.pad(keys_values, ((0, 0), (0, 0), (TILE_H, TILE_H), (0, 0), (0, 0)))
    row_list = jnp.arange(N_SEQ, dtype=jnp.int32)
    head_list = jnp.arange(HEADS, dtype=jnp.int32)
    zero_index = jnp.zeros((), jnp.int32)

    def gather_rows(row_index, head_index):
        first_row = (row_index * TILE_H).astype(jnp.int32)
        first_chan = (head_index * HEAD_DIM).astype(jnp.int32)
        q_rows = tile_order(lax.dynamic_slice(queries, (zero_index, first_row, zero_index, first_chan), (frames, TILE_H, columns, HEAD_DIM)))
        kv_rows = lax.dynamic_slice(padded_kv, (zero_index, zero_index, first_row, zero_index, first_chan), (2, frames, 3 * TILE_H, columns, HEAD_DIM))
        mask_rows = lax.dynamic_slice_in_dim(block_mask, row_index.astype(jnp.int32), 1, 1).reshape(-1, OFFSETS)
        allowed = allowed_mask(window[head_index], mask_rows, tile_coords(frames, TILE_H, columns, row_index), tile_coords(frames, 3 * TILE_H, columns, row_index - 1), N_SEQ)
        return q_rows, tile_order(kv_rows[0]), tile_order(kv_rows[1]), allowed

    def forward_head(head_index):
        def forward_row(row_index):
            q_rows, k_rows, v_rows, allowed = gather_rows(row_index, head_index)
            return head_forward(q_rows, k_rows, v_rows, allowed)
        return lax.map(forward_row, row_list)

    attended, row_max, row_sum = lax.map(forward_head, head_list)
    joined = attended.transpose(1, 2, 0, 3).reshape(N_SEQ, -1, model_width)

    def regrid(flat_rows):
        return grid_order(flat_rows, frames, TILE_H, columns)

    attn_grid = jax.vmap(regrid)(joined).transpose(1, 0, 2, 3, 4).reshape(frames, height, columns, model_width)
    attn_flat = attn_grid.reshape(-1, model_width)
    group_width = model_width // N_TENSOR
    mixed = jnp.zeros((attn_flat.shape[0], model_width), jnp.float32)
    for group in range(N_TENSOR):
        partial_value = product(attn_flat[:, group * group_width:(group + 1) * group_width], out_weight[group * group_width:(group + 1) * group_width]).astype(jnp.bfloat16)
        mixed = mixed + lax.optimization_barrier(partial_value).astype(jnp.float32)
    layer_out = mixed.astype(jnp.bfloat16).reshape(frames, height, columns, model_width)

    grad_flat = grad_out.reshape(-1, model_width)
    grad_attn = product(grad_flat, out_weight.T).astype(jnp.bfloat16).reshape(frames, height, columns, model_width)

    def add_row(row_index, carried):
        first_row = (row_index * TILE_H).astype(jnp.int32)
        attn_rows = lax.dynamic_slice_in_dim(attn_grid, first_row, TILE_H, 1).reshape(-1, model_width)
        grad_rows = lax.dynamic_slice_in_dim(grad_out, first_row, TILE_H, 1).reshape(-1, model_width)
        partial_value = product(attn_rows.T, grad_rows).astype(jnp.bfloat16)
        return carried + lax.optimization_barrier(partial_value).astype(jnp.float32)

    grad_weight = lax.fori_loop(0, N_SEQ, add_row, jnp.zeros((model_width, model_width), jnp.float32)).astype(jnp.bfloat16)

    def backward_head(inputs):
        head_index, head_max, head_sum = inputs

        def backward_row(carried, row_inputs):
            row_index, row_top, row_total = row_inputs
            q_rows, k_rows, v_rows, allowed = gather_rows(row_index, head_index)
            first_row = (row_index * TILE_H).astype(jnp.int32)
            first_chan = (head_index * HEAD_DIM).astype(jnp.int32)
            grad_rows = tile_order(lax.dynamic_slice(grad_attn, (zero_index, first_row, zero_index, first_chan), (frames, TILE_H, columns, HEAD_DIM)))
            grad_q, grad_k, grad_v = head_backward(q_rows, k_rows, v_rows, grad_rows, allowed, row_top, row_total)
            both = jnp.stack([grid_order(grad_k, frames, 3 * TILE_H, columns), grid_order(grad_v, frames, 3 * TILE_H, columns)])
            current = lax.dynamic_slice_in_dim(carried, first_row, 3 * TILE_H, 2)
            carried = lax.dynamic_update_slice_in_dim(carried, current + both, first_row, 2)
            return carried, grid_order(grad_q, frames, TILE_H, columns)

        initial = jnp.zeros((2, frames, height + 2 * TILE_H, columns, HEAD_DIM), jnp.float32)
        carried, grad_q = lax.scan(backward_row, initial, (row_list, head_max, head_sum))
        return carried[:, :, TILE_H:TILE_H + height], grad_q

    grad_kv, grad_q = lax.map(backward_head, (head_list, row_max, row_sum))
    grad_keys_values = grad_kv.transpose(1, 2, 3, 4, 0, 5).reshape(2, frames, height, columns, model_width).astype(jnp.bfloat16)
    grad_queries = grad_q.transpose(2, 1, 3, 4, 0, 5).reshape(frames, height, columns, model_width).astype(jnp.bfloat16)
    return (layer_out, grad_queries, grad_keys_values, grad_weight)
```

```python
import jax
import jax.numpy as jnp
from jax import lax
from jax.experimental import pallas as pl
from jax.experimental.pallas import tpu as pltpu
from jax.sharding import PartitionSpec as P

HEAD_DIM = 128
TILE_F = 3
TILE_H = 3
TILE_W = 8
REACH_F = 1
REACH_H = 1
REACH_W = 3
OFFSETS = 63
SCALE = HEAD_DIM**-0.5
LOG2E = 1.4426950408889634
LANES = 128
BLOCKED = -1e30
F32 = jnp.float32
BF16 = jnp.bfloat16
NT = (((1,), (1,)), ((), ()))
TN = (((0,), (0,)), ((), ()))


def mm(left, right, dims=(((1,), (0,)), ((), ()))):
    return lax.dot_general(left, right, dims, preferred_element_type=F32)


def swap(value, axis, bit):
    count = lax.axis_size(axis)
    return lax.ppermute(value, axis, [(i, i ^ bit) for i in range(count)])


def shift(value, axis, steps):
    count = lax.axis_size(axis)
    pairs = [(i, i + steps) for i in range(count) if 0 <= i + steps < count]
    return lax.ppermute(value, axis, pairs)


def turn(value, axis, steps):
    count = lax.axis_size(axis)
    return lax.ppermute(value, axis, [(i, (i + steps) % count) for i in range(count)])


def weights_of(q_ref, bias_ref, place_ref, kv_refs, onehot_ref):
    q_rows = mm(place_ref[...], q_ref[...]).astype(BF16)
    q_wide = jnp.concatenate([q_rows, bias_ref[0]], axis=1)
    scores = [
        mm(jnp.concatenate([ref[0], onehot_ref[part]], axis=1), q_wide, NT)
        for part, ref in enumerate(kv_refs)
    ]
    return q_rows, scores


def forward_kernel(q_ref, own_ref, above_ref, below_ref, bias_ref, place_ref, onehot_ref, att_ref, stat_ref):
    kv_refs = (above_ref, own_ref, below_ref)
    _, scores = weights_of(q_ref, bias_ref, place_ref, kv_refs, onehot_ref)
    tops = [jnp.max(part, axis=0, keepdims=True) for part in scores]
    top = jnp.maximum(jnp.maximum(tops[0], tops[1]), tops[2]) * (SCALE * LOG2E)
    total = jnp.zeros_like(top)
    out = jnp.zeros((HEAD_DIM, top.shape[1]), F32)
    for part, ref in zip(scores, kv_refs):
        weights = jnp.exp2(part * (SCALE * LOG2E) - top)
        total = total + jnp.sum(weights, axis=0, keepdims=True)
        out = out + mm(ref[1], weights.astype(BF16), TN)
    inverse = 1.0 / total
    att_ref[...] = (out * inverse).T.astype(BF16)
    row = lax.broadcasted_iota(jnp.int32, (8, top.shape[1]), 0)
    stat_ref[0] = jnp.where(row == 0, top, inverse)


def backward_kernel(
    q_ref, own_ref, above_ref, below_ref, bias_ref, place_ref, onehot_ref, g_ref, stat_ref,
    dq_ref, down_ref, dabove_ref, dbelow_ref,
):
    kv_refs = (above_ref, own_ref, below_ref)
    q_rows, scores = weights_of(q_ref, bias_ref, place_ref, kv_refs, onehot_ref)
    top = stat_ref[0, 0:1, :]
    inverse = stat_ref[0, 1:2, :]
    columns = top.shape[1]
    g_scaled = (g_ref[...].astype(F32).T * inverse).astype(BF16)
    weights, rounded = [], []
    out = jnp.zeros((HEAD_DIM, columns), F32)
    for part, ref in zip(scores, kv_refs):
        value = jnp.exp2(part * (SCALE * LOG2E) - top)
        weights.append(value)
        rounded.append(value.astype(BF16))
        out = out + mm(ref[1], rounded[-1], TN)
    delta = jnp.sum(out * inverse * g_scaled.astype(F32), axis=0, keepdims=True)
    high = delta.astype(BF16).astype(F32)
    row = lax.broadcasted_iota(jnp.int32, (LANES, columns), 0)
    extra = jnp.where(row == 0, -high, jnp.where(row == 1, high - delta, 0.0)).astype(BF16)
    g_wide = jnp.concatenate([g_scaled, extra], axis=0)
    keys = own_ref.shape[1]
    pick = (lax.broadcasted_iota(jnp.int32, (keys, LANES), 1) < 2).astype(F32).astype(BF16)
    dq = jnp.zeros((HEAD_DIM, columns), F32)
    for index, (ref, target) in enumerate(zip(kv_refs, (dabove_ref, down_ref, dbelow_ref))):
        inner = mm(jnp.concatenate([ref[1], pick], axis=1), g_wide)
        slope = (weights[index] * inner).astype(BF16)
        target[1] = mm(rounded[index], g_scaled, NT).astype(target.dtype)
        target[0] = (mm(slope, q_rows) * SCALE).astype(target.dtype)
        dq = dq + mm(ref[0], slope, TN)
    dq_rows = (dq * SCALE).astype(BF16).T
    dq_ref[...] = mm(place_ref[...], dq_rows, TN).astype(BF16)


def tile_bias(window, mask_rows, row_place, row_tiles, column_tiles):
    query = jnp.arange(column_tiles, dtype=jnp.int32)[:, None]
    linear = jnp.arange(3 * column_tiles, dtype=jnp.int32)[None, :]
    delta_h = linear // column_tiles - 1
    delta_w = linear % column_tiles - query
    key_row = row_place + delta_h
    offset = (REACH_F * (2 * REACH_H + 1) + delta_h + REACH_H) * (2 * REACH_W + 1) + delta_w + REACH_W
    bits = jnp.sum(
        jnp.where(
            offset[:, :, None] == jnp.arange(OFFSETS, dtype=jnp.int32), mask_rows[:, None, :], 0
        ),
        axis=-1,
    )
    kept = (bits > 0) & (jnp.abs(delta_w) <= REACH_W) & (key_row >= 0) & (key_row < row_tiles)
    reach = window[:, :, None, None]
    kept = kept & (jnp.abs(delta_h) <= reach[:, 1]) & (jnp.abs(delta_w) <= reach[:, 2])
    kept = kept & (reach[:, 0] >= 0)
    return jnp.where(kept, 0.0, BLOCKED).astype(BF16)


def shards(queries, keys_values, out_weight, grad_out, window, block_mask):
    frames, tile_rows, columns, channels = queries.shape
    model_width = grad_out.shape[3]
    local_columns = grad_out.shape[2]
    seq_count, tensor_count = lax.axis_size("seq"), lax.axis_size("tensor")
    seq_place, tensor_place = lax.axis_index("seq"), lax.axis_index("tensor")
    chips = seq_count // 2
    chip, core = seq_place // 2, seq_place % 2
    heads = channels // HEAD_DIM
    tokens = frames * tile_rows * columns
    piece = frames * tile_rows * local_columns
    slab = -(-piece // 16) * 16
    rows = tensor_count * slab
    width = model_width // seq_count

    q_flat = queries.reshape(tokens, channels)
    kv_flat = keys_values.reshape(2, tokens, channels)
    kv_above = shift(kv_flat, "seq", 1)
    kv_below = shift(kv_flat, "seq", -1)

    g_own = jnp.pad(grad_out.reshape(piece, model_width), ((0, slab - piece), (0, 0)))
    g_all = jnp.concatenate(
        [g_own] + [swap(g_own, "tensor", bit) for bit in range(1, tensor_count)], axis=0
    )

    def columns_for(place):
        return lax.dynamic_slice_in_dim(g_own, place * 2 * width, 2 * width, axis=1)

    moved = jnp.stack(
        [columns_for(chip)]
        + [
            turn(columns_for(lax.rem(chip + k, chips)), "seq", 2 * k)
            for k in range(1, chips)
        ]
    )
    kept_half = lax.dynamic_slice_in_dim(moved, core * width, width, axis=2)
    sent_half = lax.dynamic_slice_in_dim(moved, (1 - core) * width, width, axis=2)
    pair = jnp.stack([kept_half, swap(sent_half, "seq", 1)], axis=1)
    pair_all = jnp.stack(
        [pair] + [swap(pair, "tensor", bit) for bit in range(1, tensor_count)], axis=2
    ).reshape(chips, 2 * rows, width)

    row_id = jnp.arange(rows, dtype=jnp.int32)
    owner = jnp.bitwise_xor(row_id // slab, tensor_place)
    inside = row_id % slab
    column_id = owner * local_columns + inside % local_columns
    token_id = jnp.where(inside < piece, inside // local_columns * columns + column_id, -1)
    place = (token_id[:, None] == jnp.arange(tokens, dtype=jnp.int32)[None, :]).astype(BF16)
    column_tiles = columns // TILE_W
    own_mask = lax.dynamic_slice_in_dim(block_mask, seq_place, 1, 1).reshape(-1, OFFSETS)
    bias = tile_bias(window, own_mask, seq_place, seq_count, column_tiles)
    bias = jnp.pad(bias, ((0, 0), (0, 0), (0, LANES - bias.shape[2])))
    query_tile = jnp.where(inside < piece, column_id // TILE_W, -1)
    row_bias = jnp.zeros((heads, rows, LANES), BF16)
    for tile in range(column_tiles):
        row_bias = jnp.where((query_tile == tile)[None, :, None], bias[:, tile][:, None, :], row_bias)
    key_tile = (
        jnp.arange(tokens, dtype=jnp.int32)[None, :] % columns // TILE_W
        + jnp.arange(3, dtype=jnp.int32)[:, None] * column_tiles
    )
    onehot = (key_tile[:, :, None] == jnp.arange(LANES, dtype=jnp.int32)).astype(BF16)

    q_spec = pl.BlockSpec((tokens, HEAD_DIM), lambda h: (0, h))
    kv_spec = pl.BlockSpec((2, tokens, HEAD_DIM), lambda h: (0, 0, h))
    bias_spec = pl.BlockSpec((1, rows, LANES), lambda h: (h, 0, 0))
    place_spec = pl.BlockSpec((rows, tokens), lambda h: (0, 0))
    onehot_spec = pl.BlockSpec((3, tokens, LANES), lambda h: (0, 0, 0))
    row_spec = pl.BlockSpec((rows, HEAD_DIM), lambda h: (0, h))
    stat_spec = pl.BlockSpec((1, 8, rows), lambda h: (h, 0, 0))
    common = (q_spec, kv_spec, kv_spec, kv_spec, bias_spec, place_spec, onehot_spec)
    params = pltpu.CompilerParams(vmem_limit_bytes=40 * 1024 * 1024)
    work = heads * rows * tokens * 3 * HEAD_DIM * 2
    size = tokens * channels * 2

    attended, stats = pl.pallas_call(
        forward_kernel,
        grid=(heads,),
        in_specs=list(common),
        out_specs=[row_spec, stat_spec],
        out_shape=[
            jax.ShapeDtypeStruct((rows, channels), BF16),
            jax.ShapeDtypeStruct((heads, 8, rows), F32),
        ],
        compiler_params=params,
        cost_estimate=pl.CostEstimate(flops=4 * work, bytes_accessed=9 * size, transcendentals=heads * rows * tokens * 3),
        name="forward",
    )(q_flat, kv_flat, kv_above, kv_below, row_bias, place, onehot)

    ups, downs = [attended], [attended]
    for _ in range(1, chips):
        ups.append(shift(ups[-1], "seq", 2))
        downs.append(shift(downs[-1], "seq", -2))
    chunks = [attended] + [ups[k] + downs[chips - k] for k in range(1, chips)]
    grad_weight = jnp.zeros((channels, width), F32)
    for k in range(chips):
        both = jnp.concatenate([chunks[k], swap(chunks[k], "seq", 1)], axis=0)
        grad_weight = grad_weight + mm(both, pair_all[k], TN)
    grad_weight = grad_weight.astype(BF16)

    partial = mm(attended, out_weight).astype(BF16).reshape(tensor_count, slab, model_width)
    mixed = partial[0].astype(F32)
    for bit in range(1, tensor_count):
        mixed = mixed + swap(partial[bit], "tensor", bit).astype(F32)
    layer_out = mixed.astype(BF16)[:piece].reshape(frames, tile_rows, local_columns, model_width)

    grad_attn = mm(g_all, out_weight, NT).astype(BF16)
    half = jax.ShapeDtypeStruct((2, tokens, channels), BF16)
    grad_q, grad_own, grad_above, grad_below = pl.pallas_call(
        backward_kernel,
        grid=(heads,),
        in_specs=list(common) + [row_spec, stat_spec],
        out_specs=[q_spec, kv_spec, kv_spec, kv_spec],
        out_shape=[
            jax.ShapeDtypeStruct((tokens, channels), BF16),
            jax.ShapeDtypeStruct((2, tokens, channels), F32),
            half,
            half,
        ],
        compiler_params=params,
        cost_estimate=pl.CostEstimate(flops=12 * work, bytes_accessed=18 * size, transcendentals=heads * rows * tokens * 3),
        name="backward",
    )(q_flat, kv_flat, kv_above, kv_below, row_bias, place, onehot, grad_attn, stats)
    from_below = shift(grad_above, "seq", -1).astype(F32)
    from_above = shift(grad_below, "seq", 1).astype(F32)
    grad_kv = (grad_own + from_below + from_above).astype(BF16).reshape(keys_values.shape)
    return (layer_out, grad_q.reshape(queries.shape), grad_kv, grad_weight)


def solution(mesh):
    return jax.shard_map(
        shards,
        mesh=mesh,
        in_specs=(
            P(None, "seq", None, "tensor"),
            P(None, None, "seq", None, "tensor"),
            P("tensor", None),
            P(None, "seq", "tensor", None),
            P("tensor", None),
            P(),
        ),
        out_specs=(
            P(None, "seq", "tensor", None),
            P(None, "seq", None, "tensor"),
            P(None, None, "seq", None, "tensor"),
            P("tensor", "seq"),
        ),
        check_vma=False,
    )
```

```python
import jax
import jax.numpy as jnp
from jax import lax
from jax.experimental import pallas as pl
from jax.experimental.pallas import tpu as pltpu
from jax.sharding import PartitionSpec as P

HEAD_DIM = 128
TILE_F = 3
TILE_H = 3
TILE_W = 8
REACH_F = 1
REACH_H = 1
REACH_W = 3
OFFSETS = 63
SCALE = HEAD_DIM**-0.5
LOG2E = 1.4426950408889634
LANES = 128
BLOCKED = -1e30
F32 = jnp.float32
BF16 = jnp.bfloat16
NT = (((1,), (1,)), ((), ()))
TN = (((0,), (0,)), ((), ()))


def mm(left, right, dims=(((1,), (0,)), ((), ()))):
    return lax.dot_general(left, right, dims, preferred_element_type=F32)


def swap(value, axis, bit):
    count = lax.axis_size(axis)
    return lax.ppermute(value, axis, [(i, i ^ bit) for i in range(count)])


def shift(value, axis, steps):
    count = lax.axis_size(axis)
    pairs = [(i, i + steps) for i in range(count) if 0 <= i + steps < count]
    return lax.ppermute(value, axis, pairs)


def turn(value, axis, steps):
    count = lax.axis_size(axis)
    return lax.ppermute(value, axis, [(i, (i + steps) % count) for i in range(count)])


def weights_of(q_ref, bias_ref, place_ref, kv_refs, onehot_ref):
    q_rows = mm(place_ref[...], q_ref[...]).astype(BF16)
    q_wide = jnp.concatenate([q_rows, bias_ref[0]], axis=1)
    scores = [
        mm(jnp.concatenate([ref[0], onehot_ref[part]], axis=1), q_wide, NT)
        for part, ref in enumerate(kv_refs)
    ]
    return q_rows, scores


def forward_kernel(q_ref, own_ref, above_ref, below_ref, bias_ref, place_ref, onehot_ref, att_ref, stat_ref):
    kv_refs = (above_ref, own_ref, below_ref)
    _, scores = weights_of(q_ref, bias_ref, place_ref, kv_refs, onehot_ref)
    tops = [jnp.max(part, axis=0, keepdims=True) for part in scores]
    top = jnp.maximum(jnp.maximum(tops[0], tops[1]), tops[2]) * (SCALE * LOG2E)
    total = jnp.zeros_like(top)
    out = jnp.zeros((HEAD_DIM, top.shape[1]), F32)
    for part, ref in zip(scores, kv_refs):
        weights = jnp.exp2(part * (SCALE * LOG2E) - top)
        total = total + jnp.sum(weights, axis=0, keepdims=True)
        out = out + mm(ref[1], weights.astype(BF16), TN)
    inverse = 1.0 / total
    att_ref[...] = (out * inverse).T.astype(BF16)
    row = lax.broadcasted_iota(jnp.int32, (8, top.shape[1]), 0)
    stat_ref[0] = jnp.where(row == 0, top, inverse)


def backward_kernel(
    q_ref, own_ref, above_ref, below_ref, bias_ref, place_ref, onehot_ref, g_ref, stat_ref,
    dq_ref, down_ref, dabove_ref, dbelow_ref,
):
    kv_refs = (above_ref, own_ref, below_ref)
    q_rows, scores = weights_of(q_ref, bias_ref, place_ref, kv_refs, onehot_ref)
    top = stat_ref[0, 0:1, :]
    inverse = stat_ref[0, 1:2, :]
    columns = top.shape[1]
    g_scaled = (g_ref[...].astype(F32).T * inverse).astype(BF16)
    weights, rounded = [], []
    out = jnp.zeros((HEAD_DIM, columns), F32)
    for part, ref in zip(scores, kv_refs):
        value = jnp.exp2(part * (SCALE * LOG2E) - top)
        weights.append(value)
        rounded.append(value.astype(BF16))
        out = out + mm(ref[1], rounded[-1], TN)
    delta = jnp.sum(out * inverse * g_scaled.astype(F32), axis=0, keepdims=True)
    high = delta.astype(BF16).astype(F32)
    row = lax.broadcasted_iota(jnp.int32, (LANES, columns), 0)
    extra = jnp.where(row == 0, -high, jnp.where(row == 1, high - delta, 0.0)).astype(BF16)
    g_wide = jnp.concatenate([g_scaled, extra], axis=0)
    keys = own_ref.shape[1]
    pick = (lax.broadcasted_iota(jnp.int32, (keys, LANES), 1) < 2).astype(F32).astype(BF16)
    dq = jnp.zeros((HEAD_DIM, columns), F32)
    for index, (ref, target) in enumerate(zip(kv_refs, (dabove_ref, down_ref, dbelow_ref))):
        inner = mm(jnp.concatenate([ref[1], pick], axis=1), g_wide)
        slope = (weights[index] * inner).astype(BF16)
        target[1] = mm(rounded[index], g_scaled, NT).astype(target.dtype)
        target[0] = (mm(slope, q_rows) * SCALE).astype(target.dtype)
        dq = dq + mm(ref[0], slope, TN)
    dq_rows = (dq * SCALE).astype(BF16).T
    dq_ref[...] = mm(place_ref[...], dq_rows, TN).astype(BF16)


def tile_bias(window, mask_rows, row_place, row_tiles, column_tiles):
    query = jnp.arange(column_tiles, dtype=jnp.int32)[:, None]
    linear = jnp.arange(3 * column_tiles, dtype=jnp.int32)[None, :]
    delta_h = linear // column_tiles - 1
    delta_w = linear % column_tiles - query
    key_row = row_place + delta_h
    offset = (REACH_F * (2 * REACH_H + 1) + delta_h + REACH_H) * (2 * REACH_W + 1) + delta_w + REACH_W
    bits = jnp.sum(
        jnp.where(
            offset[:, :, None] == jnp.arange(OFFSETS, dtype=jnp.int32), mask_rows[:, None, :], 0
        ),
        axis=-1,
    )
    kept = (bits > 0) & (jnp.abs(delta_w) <= REACH_W) & (key_row >= 0) & (key_row < row_tiles)
    reach = window[:, :, None, None]
    kept = kept & (jnp.abs(delta_h) <= reach[:, 1]) & (jnp.abs(delta_w) <= reach[:, 2])
    kept = kept & (reach[:, 0] >= 0)
    return jnp.where(kept, 0.0, BLOCKED).astype(BF16)


def shards(queries, keys_values, out_weight, grad_out, window, block_mask):
    frames, tile_rows, columns, channels = queries.shape
    model_width = grad_out.shape[3]
    local_columns = grad_out.shape[2]
    seq_count, tensor_count = lax.axis_size("seq"), lax.axis_size("tensor")
    seq_place, tensor_place = lax.axis_index("seq"), lax.axis_index("tensor")
    chips = seq_count // 2
    chip, core = seq_place // 2, seq_place % 2
    heads = channels // HEAD_DIM
    tokens = frames * tile_rows * columns
    piece = frames * tile_rows * local_columns
    slab = -(-piece // 16) * 16
    rows = tensor_count * slab
    width = model_width // seq_count

    q_flat = queries.reshape(tokens, channels)
    kv_flat = keys_values.reshape(2, tokens, channels)
    kv_above = shift(kv_flat, "seq", 1)
    kv_below = shift(kv_flat, "seq", -1)

    g_own = jnp.pad(grad_out.reshape(piece, model_width), ((0, slab - piece), (0, 0)))
    g_pieces = [g_own] + [swap(g_own, "tensor", bit) for bit in range(1, tensor_count)]

    g_later, kv_above, kv_below = lax.optimization_barrier((g_own, kv_above, kv_below))

    def columns_for(place):
        return lax.dynamic_slice_in_dim(g_later, place * 2 * width, 2 * width, axis=1)

    moved = jnp.stack(
        [columns_for(chip)]
        + [
            turn(columns_for(lax.rem(chip + k, chips)), "seq", 2 * k)
            for k in range(1, chips)
        ]
    )
    kept_half = lax.dynamic_slice_in_dim(moved, core * width, width, axis=2)
    sent_half = lax.dynamic_slice_in_dim(moved, (1 - core) * width, width, axis=2)
    pair = jnp.stack([kept_half, swap(sent_half, "seq", 1)], axis=1)
    pair_all = jnp.stack(
        [pair] + [swap(pair, "tensor", bit) for bit in range(1, tensor_count)], axis=2
    ).reshape(chips, 2 * rows, width)

    row_id = jnp.arange(rows, dtype=jnp.int32)
    owner = jnp.bitwise_xor(row_id // slab, tensor_place)
    inside = row_id % slab
    column_id = owner * local_columns + inside % local_columns
    token_id = jnp.where(inside < piece, inside // local_columns * columns + column_id, -1)
    place = (token_id[:, None] == jnp.arange(tokens, dtype=jnp.int32)[None, :]).astype(BF16)
    column_tiles = columns // TILE_W
    own_mask = lax.dynamic_slice_in_dim(block_mask, seq_place, 1, 1).reshape(-1, OFFSETS)
    bias = tile_bias(window, own_mask, seq_place, seq_count, column_tiles)
    bias = jnp.pad(bias, ((0, 0), (0, 0), (0, LANES - bias.shape[2])))
    query_tile = jnp.where(inside < piece, column_id // TILE_W, -1)
    row_bias = jnp.zeros((heads, rows, LANES), BF16)
    for tile in range(column_tiles):
        row_bias = jnp.where((query_tile == tile)[None, :, None], bias[:, tile][:, None, :], row_bias)
    key_tile = (
        jnp.arange(tokens, dtype=jnp.int32)[None, :] % columns // TILE_W
        + jnp.arange(3, dtype=jnp.int32)[:, None] * column_tiles
    )
    onehot = (key_tile[:, :, None] == jnp.arange(LANES, dtype=jnp.int32)).astype(BF16)

    q_spec = pl.BlockSpec((tokens, HEAD_DIM), lambda h: (0, h))
    kv_spec = pl.BlockSpec((2, tokens, HEAD_DIM), lambda h: (0, 0, h))
    bias_spec = pl.BlockSpec((1, rows, LANES), lambda h: (h, 0, 0))
    place_spec = pl.BlockSpec((rows, tokens), lambda h: (0, 0))
    onehot_spec = pl.BlockSpec((3, tokens, LANES), lambda h: (0, 0, 0))
    row_spec = pl.BlockSpec((rows, HEAD_DIM), lambda h: (0, h))
    stat_spec = pl.BlockSpec((1, 8, rows), lambda h: (h, 0, 0))
    common = (q_spec, kv_spec, kv_spec, kv_spec, bias_spec, place_spec, onehot_spec)
    params = pltpu.CompilerParams(vmem_limit_bytes=40 * 1024 * 1024)
    work = heads * rows * tokens * 3 * HEAD_DIM * 2
    size = tokens * channels * 2

    attended, stats = pl.pallas_call(
        forward_kernel,
        grid=(heads,),
        in_specs=list(common),
        out_specs=[row_spec, stat_spec],
        out_shape=[
            jax.ShapeDtypeStruct((rows, channels), BF16),
            jax.ShapeDtypeStruct((heads, 8, rows), F32),
        ],
        compiler_params=params,
        cost_estimate=pl.CostEstimate(flops=4 * work, bytes_accessed=9 * size, transcendentals=heads * rows * tokens * 3),
        name="forward",
    )(q_flat, kv_flat, kv_above, kv_below, row_bias, place, onehot)

    ups, downs = [attended], [attended]
    for _ in range(1, chips):
        up, down = lax.optimization_barrier((ups[-1], downs[-1]))
        ups.append(shift(up, "seq", 2))
        downs.append(shift(down, "seq", -2))
    chunks = [attended] + [ups[k] + downs[chips - k] for k in range(1, chips)]
    grad_weight = jnp.zeros((channels, width), F32)
    for k in range(chips):
        both = jnp.concatenate([chunks[k], swap(chunks[k], "seq", 1)], axis=0)
        grad_weight = grad_weight + mm(both, pair_all[k], TN)
    grad_weight = grad_weight.astype(BF16)

    first, last = min(1, chips - 1), min(2, chips - 1)
    *g_pieces, _ = lax.optimization_barrier((*g_pieces, attended))
    grad_attn = mm(jnp.concatenate(g_pieces, axis=0), out_weight, NT).astype(BF16)
    attended, _, _ = lax.optimization_barrier((attended, ups[first], downs[first]))
    partial = mm(attended, out_weight).astype(BF16).reshape(tensor_count, slab, model_width)
    mixed = partial[0].astype(F32)
    for bit in range(1, tensor_count):
        mixed = mixed + swap(partial[bit], "tensor", bit).astype(F32)
    layer_out = mixed.astype(BF16)[:piece].reshape(frames, tile_rows, local_columns, model_width)

    half = jax.ShapeDtypeStruct((2, tokens, channels), BF16)
    grad_shapes = [
        jax.ShapeDtypeStruct((tokens, channels), BF16),
        jax.ShapeDtypeStruct((2, tokens, channels), F32),
        half,
        half,
    ]

    def backward(first_head, count, stats, grads):
        def moved_spec(spec):
            index_map = spec.index_map
            return pl.BlockSpec(spec.block_shape, lambda h: index_map(h + first_head))

        def body(*refs):
            backward_kernel(*refs[:9], *refs[9 + len(grads) :])

        specs = list(common) + [row_spec, stat_spec]
        return pl.pallas_call(
            body,
            grid=(count,),
            in_specs=[moved_spec(spec) for spec in specs]
            + [pl.BlockSpec(memory_space=pl.ANY)] * len(grads),
            out_specs=[moved_spec(spec) for spec in (q_spec, kv_spec, kv_spec, kv_spec)],
            out_shape=grad_shapes,
            input_output_aliases={9 + i: i for i in range(len(grads))},
            compiler_params=params,
            cost_estimate=pl.CostEstimate(
                flops=12 * work * count // heads,
                bytes_accessed=18 * size * count // heads,
                transcendentals=count * rows * tokens * 3,
            ),
            name="backward",
        )(q_flat, kv_flat, kv_above, kv_below, row_bias, place, onehot, grad_attn, stats, *grads)

    cut = heads // 2
    stats, _, _ = lax.optimization_barrier((stats, ups[first], downs[first]))
    grads = backward(0, cut, stats, ())
    stats, _, _ = lax.optimization_barrier((stats, ups[last], downs[last]))
    grad_q, grad_own, grad_above, grad_below = backward(cut, heads - cut, stats, tuple(grads))
    grad_above, grad_below, _, _ = lax.optimization_barrier(
        (grad_above, grad_below, ups[-1], downs[-1])
    )
    from_below = shift(grad_above, "seq", -1).astype(F32)
    from_above = shift(grad_below, "seq", 1).astype(F32)
    grad_kv = (grad_own + from_below + from_above).astype(BF16).reshape(keys_values.shape)
    return (layer_out, grad_q.reshape(queries.shape), grad_kv, grad_weight)


def solution(mesh):
    return jax.shard_map(
        shards,
        mesh=mesh,
        in_specs=(
            P(None, "seq", None, "tensor"),
            P(None, None, "seq", None, "tensor"),
            P("tensor", None),
            P(None, "seq", "tensor", None),
            P("tensor", None),
            P(),
        ),
        out_specs=(
            P(None, "seq", "tensor", None),
            P(None, "seq", None, "tensor"),
            P(None, None, "seq", None, "tensor"),
            P("tensor", "seq"),
        ),
        check_vma=False,
    )
```
